512 devices in a mesh: dp: 32 (over x, y, core), expert: 16 (over z).
Axes of the slice: x: 4, y: 4, z: 16, core: 2. Of those that a mesh axis runs over, the one named last changes fastest.
Arguments:
- grad_out: bfloat16 [2048, 6144], P('expert', 'dp'), may hold values from -48 to 48
- routes: int32 [2048, 4], P('expert'), may hold values from 0 to 15, all different within a row; in each aligned block of 128 rows (0 to 127, 128 to 255, ...) at most 40 rows name the same one
- probs: float32 [2048, 4], P('expert'), may hold values from 0.05 to 0.6
- resp_len: int32 [16, 4], P('expert'), may hold values from 1 to 64, 128 in all within a row
- w_down: bfloat16 [16, 5376, 6144], P('expert', 'dp'), may hold values from -0.078125 to 0.078125
- w_up: bfloat16 [16, 6144, 5376], P('expert', 'dp'), may hold values from -0.078125 to 0.078125
- gate_act: bfloat16 [16, 640, 5376], P('expert', None, 'dp'), may hold values from -6 to 6
Outputs:
- grad_in: bfloat16 [2048, 6144], P('expert', 'dp')
The draws below stay inside these ranges and needn't reach their ends.
Inputs may be any that keep to these rules, and one draw needn't show every extreme that they name: `routes`: within each aligned block of 128 rows (one shard) no expert is named more than 40 times, a bound that some block reaches. `resp_len`: each row sums to 128, and its largest entry is 64.
All inputs are finite; a program needn't handle non-finite values.
Results may differ from the reference program's by a relative error of at most 0.013.
Values may be sent and summed in bfloat16 or wider, within the bound.
No kernel may reach another device: no remote copies, remote signals or barrier semaphores. Data moves between devices by JAX's collectives and lax.ppermute only.
A program may use at most 64 MiB of HBM per device.

```python
import math
import jax
import jax.numpy as jnp
import numpy as np
from jax import lax

D = 6144
TOP = 4
HID = 5376
RESP = 4
TOK_DEV = 128
EXPERTS = 16
CAP = 40
SLOTS = 640
TOKENS = 2048
N_EXPERT = 16


def levels(stream_key, extent, split, smallest, top_value):
    loudness, own = 1.0, jax.random.fold_in(stream_key, 6)
    for dim, shards_of in split:
        steps = jnp.exp(jax.random.uniform(jax.random.fold_in(own, dim), (shards_of,), jnp.float32, smallest / len(split), top_value / len(split)))
        loudness = loudness * jnp.repeat(steps, extent[dim] // shards_of).reshape([-1 if axis == dim else 1 for axis in range(len(extent))])
    return loudness


def profile(number_of, total, limit, slope):
    loads = [(1 << 20) // math.isqrt(rank ** slope) + 1 for rank in range(2, number_of + 1)]
    rest, holding = total - limit - (number_of - 1), [1] * (number_of - 1)
    while rest > 0:
        free = [i for i in range(number_of - 1) if holding[i] < limit]
        whole, budget = sum([loads[i] for i in free]), rest
        for i in free:
            more = min(limit - holding[i], max(1, budget * loads[i] // whole), rest)
            holding[i] = holding[i] + more
            rest = rest - more
    return np.array([limit] + holding)


def uneven(key, number_of, total, reach, lean):
    if number_of == 2:
        one = jax.random.randint(key, (), max(1, total - reach), min(reach, total - 1) + 1)
        return jnp.stack([one, total - one])
    sizes = jnp.asarray(profile(number_of, total, reach, lean), jnp.int32)
    couples = (number_of - 1) // 2
    giver, receiver = sizes[1:1 + 2 * couples:2], sizes[2:2 + 2 * couples:2]
    margin = jnp.minimum(giver - 1, reach - receiver)
    shifted = jax.random.randint(jax.random.fold_in(key, 1), (couples,), 0, 1 << 20) % (margin + 1)
    sizes = sizes.at[1:1 + 2 * couples:2].set(giver - shifted).at[2:2 + 2 * couples:2].set(receiver + shifted)
    return sizes[jax.random.permutation(jax.random.fold_in(key, 2), number_of)]


def routed_block(stream_key, own, number, rows, amount, top, reach, lean):
    order = jax.random.permutation(stream_key, amount)
    packed, ordinary = portions_of(amount, rows * top, reach, lean, True), portions_of(amount, rows * top, reach, lean, False)
    places = jnp.arange(amount)

    def named(sizes, offset_by):
        used = int((sizes > 0).sum())
        fixed = max(1, used // 4)
        moved = fixed + (places - fixed + offset_by * (used - fixed)) % max(1, amount - fixed)
        return jnp.zeros((amount,), jnp.int32).at[order[jnp.where(places < fixed, places, moved)]].set(jnp.asarray(sizes, jnp.int32))

    sizes = jnp.where(number % 4 == 0, named(packed, number // 4), named(ordinary, number - number // 4 - 1))
    mixed = jax.random.permutation(jax.random.fold_in(own, 3), amount)
    giver, sink = mixed[0:amount // 2 * 2:2], mixed[1:amount // 2 * 2:2]
    room = jnp.minimum(sizes[giver] - 1, reach - sizes[sink]) // 2
    room = jnp.where((giver == order[0]) | (sink == order[0]) | (sizes[sink] == 0), 0, jnp.maximum(room, 0))
    moved = jax.random.randint(jax.random.fold_in(own, 4), (amount // 2,), 0, 1 << 20) % (room + 1)
    sizes = sizes.at[giver].add(-moved).at[sink].add(moved)
    items = jnp.searchsorted(jnp.cumsum(sizes), jnp.arange(rows * top), side="right").astype(jnp.int32)
    listing = items.reshape(top, rows).T
    listing = listing[jax.random.permutation(jax.random.fold_in(own, 1), rows)]
    offset_by = jax.random.randint(jax.random.fold_in(own, 2), (rows, 1), 0, top)
    return jnp.take_along_axis(listing, (jnp.arange(top)[None, :] + offset_by) % top, axis=1)


def portions_of(amount, total, limit, slope, full):
    portions = [(1 << 20) // math.isqrt(standing ** slope) + 1 for standing in range(1, amount + 1)]
    largest = limit if full else min(limit, max(-(-total // amount), total * portions[0] // sum(portions)))
    least = 1 if total - largest >= amount - 1 else 0
    given, surplus = [largest] + [least] * (amount - 1), total - largest - least * (amount - 1)
    while surplus > 0:
        free = [i for i in range(1, amount) if given[i] < largest] or [i for i in range(1, amount) if given[i] < limit]
        mass, budget = sum([portions[i] for i in free]), surplus
        for i in free:
            extra = min(limit - given[i], max(1, budget * portions[i] // mass), surplus)
            given[i] = given[i] + extra
            surplus = surplus - extra
    return np.array(given)


def bell_draw(key, dims, scale, bound, cuts=(), kind=jnp.bfloat16):
    factor_of = levels(key, dims, cuts, -0.22, 0.18) if cuts else 1.0
    array = jax.random.normal(key, dims, jnp.float32) * scale * factor_of
    return jnp.minimum(jnp.maximum(array, -bound), bound).astype(kind)


def setup_inputs(seed: int = 0) -> dict:
    keys = jax.random.split(jax.random.key(seed), 8)
    grad_out = bell_draw(keys[0], (TOKENS, D), 8.0, 48.0, ((0, 16), (1, 32)))
    routes_keys = jax.random.split(jax.random.fold_in(keys[1], 1), TOKENS // TOK_DEV)
    routes_turns = jax.random.permutation(jax.random.fold_in(keys[1], 3), TOKENS // TOK_DEV)
    routes = jax.vmap(lambda own, number: routed_block(jax.random.fold_in(keys[1], 2), own, number, TOK_DEV, EXPERTS, TOP, CAP, 2))(routes_keys, routes_turns).reshape((TOKENS, TOP))
    probs = jnp.clip(0.05 + 0.55 * jax.random.uniform(keys[2], (TOKENS, TOP), jnp.float32) ** levels(keys[2], (TOKENS, TOP), ((0, 16),), -0.2, 0.2), 0.05, 0.6)
    resp_len = jax.vmap(lambda own: uneven(own, RESP, TOK_DEV, TOK_DEV // 2, 2))(jax.random.split(keys[3], N_EXPERT)).reshape((N_EXPERT, RESP)).astype(jnp.int32)
    w_down = bell_draw(keys[4], (EXPERTS, HID, D), D ** -0.5, 0.078125, ((0, 16), (1, 32)))
    w_up = bell_draw(keys[5], (EXPERTS, D, HID), HID ** -0.5, 0.078125, ((0, 16), (1, 32)))
    gate_act = bell_draw(keys[6], (EXPERTS, SLOTS, HID), 1.0, 6.0, ((0, 16), (2, 32)))
    return dict(grad_out=grad_out, routes=routes, probs=probs, resp_len=resp_len, w_down=w_down, w_up=w_up, gate_act=gate_act)


def token_weight(resp_len, rows):
    lengths = resp_len[0]
    ends = jnp.cumsum(lengths)
    starts = ends - lengths
    position = jnp.arange(rows, dtype=jnp.int32)[:, None]
    inside = (position >= starts[None, :]) & (position < ends[None, :])
    inverse = 1.0 / lengths.astype(jnp.float32)
    return jnp.sum(jnp.where(inside, inverse[None, :], jnp.zeros_like(inverse)[None, :]), axis=1)


def slot_index(routes, experts, capacity):
    labels = jnp.arange(experts, dtype=jnp.int32)
    hits = (routes[:, :, None] == labels[None, None, :]).astype(jnp.int32)
    per_row = jnp.sum(hits, axis=1)
    before = jnp.cumsum(per_row, axis=0) - per_row
    position = jnp.sum(hits * before[:, None, :], axis=2)
    return (routes * capacity + position).astype(jnp.int32)


def reference(grad_out, routes, probs, resp_len, w_down, w_up, gate_act):
    grad_shards = grad_out.reshape(N_EXPERT, TOK_DEV, D)
    route_shards = routes.reshape(N_EXPERT, TOK_DEV, TOP)
    prob_shards = probs.reshape(N_EXPERT, TOK_DEV, TOP)

    def dispatch(shard_grad, shard_routes, shard_probs, shard_len):
        weight = token_weight(shard_len[None, :], TOK_DEV)
        target = slot_index(shard_routes, EXPERTS, CAP).reshape(-1)
        factor = shard_probs * weight[:, None]
        scaled = (shard_grad[:, None, :].astype(jnp.float32) * factor[:, :, None]).astype(jnp.bfloat16)
        placed = jnp.zeros((EXPERTS * CAP, D), jnp.bfloat16).at[target].set(scaled.reshape(TOK_DEV * TOP, D))
        return placed, target

    outgoing, targets = jax.vmap(dispatch)(grad_shards, route_shards, prob_shards, resp_len)
    arrived = outgoing.reshape(N_EXPERT, EXPERTS, CAP, D).transpose(1, 0, 2, 3).reshape(EXPERTS, SLOTS, D)

    def expert_grads(operands):
        inputs, down_rows, up_rows, saved = operands
        total = lax.dot_general(inputs, down_rows, (((1,), (1,)), ((), ())), preferred_element_type=jnp.float32)
        hidden_grad = (total * saved.astype(jnp.float32)).astype(jnp.bfloat16)
        product = lax.dot_general(hidden_grad, up_rows, (((1,), (1,)), ((), ())), preferred_element_type=jnp.float32)
        return product.astype(jnp.bfloat16)

    returning = lax.map(expert_grads, (arrived, w_down, w_up, gate_act))
    back = returning.reshape(EXPERTS, N_EXPERT, CAP, D).transpose(1, 0, 2, 3).reshape(N_EXPERT, EXPERTS * CAP, D)

    def combine(shard_back, target):
        picked = jnp.take(shard_back, target, axis=0).reshape(TOK_DEV, TOP, D).astype(jnp.float32)
        return jnp.sum(picked, axis=1).astype(jnp.bfloat16)

    return jax.vmap(combine)(back, targets).reshape(TOKENS, D)
```

```python
import functools

import jax
import jax.numpy as jnp
from jax import lax
from jax.experimental import pallas as pl
from jax.experimental.pallas import tpu as pltpu
from jax.sharding import PartitionSpec as P

SIDE = 4
CORES = 2
EXPERTS = 16
CAPACITY = 40
SLOTS = EXPERTS * CAPACITY
LANES = 128
PIECES = LANES // CAPACITY
MIB = 1 << 20
MOST = 58 * MIB


def index(x, y, c):
    return ((x % SIDE) * SIDE + y % SIDE) * CORES + c


X_GROUPS = [[index(x, y, c) for x in range(SIDE)] for y in range(SIDE) for c in range(CORES)]
Y_GROUPS = [[index(x, y, c) for y in range(SIDE)] for x in range(SIDE) for c in range(CORES)]


def moves(dx, dy, swap=0):
    return [
        (index(x, y, c), index(x + dx, y + dy, (c + swap) % CORES))
        for x in range(SIDE)
        for y in range(SIDE)
        for c in range(CORES)
    ]


OTHER_CORE = moves(0, 0, 1)


def exchange(blocks, groups):
    return lax.all_to_all(blocks, "dp", 0, 0, tiled=True, axis_index_groups=groups)


def after(value, *others):
    return lax.optimization_barrier((value, *others))[0]


def call(kernel, out_shape, n_scalars, n_arrays, limit=6 * MIB, scratch=(), flops=0, moved=0):
    return pl.pallas_call(
        kernel,
        out_shape=out_shape,
        in_specs=[pl.BlockSpec(memory_space=pltpu.SMEM)] * n_scalars
        + [pl.BlockSpec(memory_space=pltpu.VMEM)] * n_arrays,
        out_specs=jax.tree.map(lambda _: pl.BlockSpec(memory_space=pltpu.VMEM), out_shape),
        scratch_shapes=scratch,
        compiler_params=pltpu.CompilerParams(vmem_limit_bytes=limit),
        cost_estimate=pl.CostEstimate(flops=flops, bytes_accessed=moved, transcendentals=0),
    )


def iota(shape, dim):
    return lax.broadcasted_iota(jnp.int32, shape, dim)


def pieces(shape, dim=1):
    at = iota(shape, dim)
    piece = jnp.zeros(shape, jnp.int32)
    for i in range(1, PIECES + 1):
        piece = piece + jnp.where(at >= i * CAPACITY, 1, 0)
    return piece, at - piece * CAPACITY


def held_slots(tokens):
    piece, within = pieces((LANES, tokens), 0)
    return jnp.where(piece < PIECES, within, -2).astype(jnp.float32)


def dispatch_kernel(lengths, routes_ref, probs_ref, grad_ref, out_ref, slot_ref):
    width, tokens = grad_ref.shape
    at = iota((1, tokens), 1)
    weight = jnp.zeros((1, tokens), jnp.float32)
    start = jnp.int32(0)
    for i in range(lengths.shape[1]):
        length = lengths[0, i]
        inverse = 1.0 / jnp.full((1, tokens), length, jnp.int32).astype(jnp.float32)
        weight = weight + jnp.where((at >= start) & (at < start + length), inverse, 0.0)
        start = start + length

    label = iota((EXPERTS, tokens), 0)
    hits = jnp.zeros((EXPERTS, tokens), jnp.float32)
    factor = jnp.zeros((EXPERTS, tokens), jnp.float32)
    for k in range(routes_ref.shape[0]):
        named = routes_ref[k : k + 1, :] == label
        hits = hits + jnp.where(named, 1.0, 0.0)
        factor = factor + jnp.where(named, probs_ref[k : k + 1, :] * weight, 0.0)
    above = (iota((tokens, tokens), 0) < iota((tokens, tokens), 1)).astype(jnp.bfloat16)
    before = jnp.dot(hits.astype(jnp.bfloat16), above, preferred_element_type=jnp.float32)
    slot = jnp.where(hits > 0.0, before, -1.0)
    slot_ref[...] = slot

    piece, _ = pieces((1, LANES))
    held = held_slots(tokens)
    chunk = width // PIECES
    source = grad_ref[...].astype(jnp.float32)
    for e in range(EXPERTS):
        pick = jnp.where(slot[e : e + 1, :] == held, 1.0, 0.0).astype(jnp.bfloat16)
        scaled = (source * factor[e : e + 1, :]).astype(jnp.bfloat16)
        full = lax.dot_general(scaled, pick, (((1,), (1,)), ((), ())), preferred_element_type=jnp.float32)
        chosen = full[0:chunk]
        for q in range(1, PIECES):
            chosen = jnp.where(piece == q, full[q * chunk : (q + 1) * chunk], chosen)
        out_ref[e] = chosen.astype(jnp.bfloat16)


def unpack_kernel(in_ref, out_ref):
    shards, chunk, _ = in_ref.shape
    blocks = [in_ref[s].astype(jnp.float32) for s in range(shards)]
    lane = iota((1, LANES), 1)
    for q in range(PIECES):
        turned = [
            pltpu.roll(blocks[s], ((s - q) * CAPACITY) % LANES, 1) if ((s - q) * CAPACITY) % LANES else blocks[s]
            for s in range(shards)
        ]
        for b in range(SLOTS // LANES):
            block = jnp.zeros((chunk, LANES), jnp.float32)
            for s in range(shards):
                low = max(s * CAPACITY - b * LANES, 0)
                high = min((s + 1) * CAPACITY - b * LANES, LANES)
                if low < high:
                    block = jnp.where((lane >= low) & (lane < high), turned[s], block)
            block = block.astype(jnp.bfloat16)
            for n in range(out_ref.shape[0]):
                out_ref[n, q * chunk : (q + 1) * chunk, b * LANES : (b + 1) * LANES] = block


def product_kernel(along, copied, place, own_ref, other_ref, *refs):
    weights, out_ref, data = refs[:SIDE], refs[SIDE], refs[SIDE + 1]
    copies = []
    if copied:
        held, sems = refs[SIDE + 2 : -1], refs[-1]
        copies = [pltpu.make_async_copy(weights[k], held[k], sems.at[k]) for k in range(SIDE)]
        weights = held
    for copy in copies:
        copy.start()
    deep = own_ref.shape[1]
    for core in range(CORES):

        @pl.when(place[2] == core)
        def _(core=core):
            both = (own_ref, other_ref) if core == 0 else (other_ref, own_ref)
            for n in range(SIDE):
                data[2 * n * deep : 2 * (n + 1) * deep, :] = jnp.concatenate([ref[n] for ref in both], axis=0)

    for k in range(SIDE):
        if copied:
            copies[k].wait()
        part = jnp.dot(weights[k][...], data[...], preferred_element_type=jnp.float32)
        out_ref[lax.rem(place[along] + SIDE - k, SIDE)] = part.astype(jnp.bfloat16)


def added(in_ref):
    total = in_ref[0].astype(jnp.float32)
    for n in range(1, in_ref.shape[0]):
        total = total + in_ref[n].astype(jnp.float32)
    return total


def gate_kernel(in_ref, gate_ref, out_ref):
    hidden = (added(in_ref) * gate_ref[...].astype(jnp.float32)).astype(jnp.bfloat16)
    for n in range(out_ref.shape[0]):
        out_ref[n] = hidden


def pack_kernel(in_ref, out_ref):
    shards, chunk, _ = out_ref.shape
    total = added(in_ref)
    piece, _ = pieces((1, LANES))
    lane = iota((1, LANES), 1)
    for s in range(shards):
        b, low = divmod(s * CAPACITY, LANES)
        block = jnp.zeros((chunk, LANES), jnp.float32)
        for q in range(PIECES):
            rows = total[q * chunk : (q + 1) * chunk]
            part = rows[:, b * LANES : (b + 1) * LANES]
            if low + CAPACITY > LANES:
                part = jnp.where(lane >= low, part, rows[:, (b + 1) * LANES : (b + 2) * LANES])
            turn = (q * CAPACITY - low) % LANES
            block = jnp.where(piece == q, pltpu.roll(part, turn, 1) if turn else part, block)
        out_ref[s] = block.astype(jnp.bfloat16)


def combine_kernel(in_ref, slot_ref, out_ref):
    piece, _ = pieces((1, LANES))
    held = held_slots(slot_ref.shape[1])
    total = jnp.zeros(out_ref.shape, jnp.float32)
    for e in range(in_ref.shape[0]):
        block = in_ref[e].astype(jnp.float32)
        spread = jnp.concatenate([jnp.where(piece == q, block, 0.0) for q in range(PIECES)], axis=0)
        pick = jnp.where(slot_ref[e : e + 1, :] == held, 1.0, 0.0).astype(jnp.bfloat16)
        total = total + jnp.dot(spread.astype(jnp.bfloat16), pick, preferred_element_type=jnp.float32)
    out_ref[...] = total.astype(jnp.bfloat16)


def cut_down_kernel(place, in_ref, *refs):
    out_refs, held, into, out_of = refs[:SIDE], refs[SIDE : 2 * SIDE], refs[-2], refs[-1]
    wide = in_ref.shape[1] // (SIDE * SIDE)

    def taken(k, n):
        block = n * SIDE + lax.rem(place[1] + k, SIDE)
        return pltpu.make_async_copy(
            in_ref.at[:, pl.ds(pl.multiple_of(block * wide, wide), wide)],
            held[k].at[:, pl.ds(n * wide, wide)],
            into.at[k, n],
        )

    def given(k):
        return pltpu.make_async_copy(held[k], out_refs[k], out_of.at[k])

    order = (1, 3, 2, 0)
    for k in order:
        for n in range(SIDE):
            taken(k, n).start()
    for k in order:
        for n in range(SIDE):
            taken(k, n).wait()
        given(k).start()
    for k in order:
        given(k).wait()


def cut_up_kernel(place, in_ref, *refs):
    out_refs, whole, held, into, out_of = refs[:SIDE], refs[SIDE], refs[SIDE + 1 : -2], refs[-2], refs[-1]
    fetch = pltpu.make_async_copy(in_ref, whole, into)
    fetch.start()
    fetch.wait()
    wide = in_ref.shape[1] // SIDE
    for at in range(SIDE):

        @pl.when(place[0] == at)
        def _(at=at):
            for k in range(SIDE):
                n = (at + k) % SIDE
                held[k][...] = whole[:, n * wide : (n + 1) * wide]

    copies = [pltpu.make_async_copy(held[k], out_refs[k], out_of.at[k]) for k in range(SIDE)]
    for copy in copies:
        copy.start()
    for copy in copies:
        copy.wait()


def cut(kernel, place, weights, whole, sems):
    part = jax.ShapeDtypeStruct((weights.shape[0], weights.shape[1] // SIDE), weights.dtype)
    in_hbm = pl.BlockSpec(memory_space=pltpu.HBM)
    return list(
        pl.pallas_call(
            kernel,
            out_shape=[part] * SIDE,
            in_specs=[pl.BlockSpec(memory_space=pltpu.SMEM), in_hbm],
            out_specs=[in_hbm] * SIDE,
            scratch_shapes=[pltpu.VMEM(weights.shape, weights.dtype)] * whole
            + [pltpu.VMEM(part.shape, part.dtype)] * SIDE
            + [pltpu.SemaphoreType.DMA(shape) for shape in sems],
            compiler_params=pltpu.CompilerParams(vmem_limit_bytes=MOST),
        )(place, weights)
    )


def send(part, dx, dy):
    return lax.ppermute(part, "dp", moves(dx, dy))


def product(along, copied, place, rows, weights):
    other = lax.ppermute(rows, "dp", OTHER_CORE)
    _, deep, slots = rows.shape
    in_vmem = pl.BlockSpec(memory_space=pltpu.VMEM)
    scratch = [pltpu.VMEM((CORES * SIDE * deep, slots), jnp.bfloat16)]
    if copied:
        scratch += [pltpu.VMEM(part.shape, part.dtype) for part in weights]
        scratch += [pltpu.SemaphoreType.DMA((SIDE,))]
    return pl.pallas_call(
        functools.partial(product_kernel, along, copied),
        out_shape=jax.ShapeDtypeStruct((SIDE, weights[0].shape[0], slots), jnp.bfloat16),
        in_specs=[pl.BlockSpec(memory_space=pltpu.SMEM)]
        + [in_vmem] * 2
        + [pl.BlockSpec(memory_space=pltpu.HBM) if copied else in_vmem] * SIDE,
        out_specs=in_vmem,
        scratch_shapes=scratch,
        compiler_params=pltpu.CompilerParams(vmem_limit_bytes=MOST if copied else 12 * MIB),
    )(place, rows, other, *weights)


def on_device(grad_out, routes, probs, resp_len, w_down, w_up, gate_act):
    tokens, width = grad_out.shape
    hidden = w_down.shape[1]
    chunk = width // PIECES
    me = lax.axis_index("dp")
    place = jnp.stack([me // (SIDE * CORES), (me // CORES) % SIDE, me % CORES]).astype(jnp.int32)

    def half(*shape):
        return jax.ShapeDtypeStruct(shape, jnp.bfloat16)

    outgoing, slots = call(
        dispatch_kernel, (half(EXPERTS, chunk, LANES), jax.ShapeDtypeStruct((EXPERTS, tokens), jnp.float32)), 1, 3
    )(resp_len, routes.T, probs.T, grad_out.T)
    together = lax.optimization_barrier

    down = cut(cut_down_kernel, place, w_down[0], 0, [(SIDE, SIDE), (SIDE,)])
    outgoing, down = together((outgoing, down))
    arrived = lax.all_to_all(outgoing, "expert", 0, 0, tiled=True)
    arrived, down[1], down[3] = together((arrived, send(down[1], 0, 1), send(down[3], 0, 3)))

    spread = call(unpack_kernel, half(SIDE, width, SLOTS), 0, 1)(arrived)
    spread, down[2], up = together((spread, down[2], w_up[0]))
    rows = exchange(spread, X_GROUPS)
    up = cut(cut_up_kernel, place, up, 1, [(), (SIDE,)])
    rows, down[2], up = together((rows, send(down[2], 0, 2), up))

    partial = product(1, True, place, rows, down)
    partial, up = together((partial, up))
    sums = exchange(partial, Y_GROUPS)
    sums, up[1], up[3] = together((sums, send(up[1], 1, 0), send(up[3], 3, 0)))
    spread = call(gate_kernel, half(SIDE, hidden, SLOTS), 0, 2)(sums, gate_act[0].T)
    spread, up[2] = together((spread, up[2]))
    rows = exchange(spread, Y_GROUPS)
    rows, up[2] = together((rows, send(up[2], 2, 0)))
    partial = product(0, False, place, rows, up)
    returning = call(pack_kernel, half(EXPERTS, chunk, LANES), 0, 1)(exchange(partial, X_GROUPS))
    back = lax.all_to_all(returning, "expert", 0, 0, tiled=True)
    return call(combine_kernel, half(width, tokens), 0, 2)(back, slots).T


def solution(mesh):
    in_specs = (
        P("expert", "dp"),
        P("expert", None),
        P("expert", None),
        P("expert", None),
        P("expert", "dp", None),
        P("expert", "dp", None),
        P("expert", None, "dp"),
    )
    out_specs = P("expert", "dp")
    return jax.shard_map(
        on_device, mesh=mesh, in_specs=in_specs, out_specs=out_specs, check_vma=False
    )
```

```python
import functools

import jax
import jax.numpy as jnp
from jax import lax
from jax.experimental import pallas as pl
from jax.experimental.pallas import tpu as pltpu
from jax.sharding import PartitionSpec as P

SIDE = 4
CORES = 2
EXPERTS = 16
CAPACITY = 40
SLOTS = EXPERTS * CAPACITY
LANES = 128
PIECES = LANES // CAPACITY
MIB = 1 << 20
MOST = 58 * MIB


def index(x, y, c):
    return ((x % SIDE) * SIDE + y % SIDE) * CORES + c


X_GROUPS = [[index(x, y, c) for x in range(SIDE)] for y in range(SIDE) for c in range(CORES)]
Y_GROUPS = [[index(x, y, c) for y in range(SIDE)] for x in range(SIDE) for c in range(CORES)]


def moves(dx, dy, swap=0):
    return [
        (index(x, y, c), index(x + dx, y + dy, (c + swap) % CORES))
        for x in range(SIDE)
        for y in range(SIDE)
        for c in range(CORES)
    ]


OTHER_CORE = moves(0, 0, 1)


def exchange(blocks, groups):
    return lax.all_to_all(blocks, "dp", 0, 0, tiled=True, axis_index_groups=groups)


def gather(block, groups):
    return lax.all_gather(block, "dp", axis_index_groups=groups)


def after(value, *others):
    return lax.optimization_barrier((value, *others))[0]


def call(kernel, out_shape, n_scalars, n_arrays, limit=6 * MIB, scratch=(), flops=0, moved=0):
    return pl.pallas_call(
        kernel,
        out_shape=out_shape,
        in_specs=[pl.BlockSpec(memory_space=pltpu.SMEM)] * n_scalars
        + [pl.BlockSpec(memory_space=pltpu.VMEM)] * n_arrays,
        out_specs=jax.tree.map(lambda _: pl.BlockSpec(memory_space=pltpu.VMEM), out_shape),
        scratch_shapes=scratch,
        compiler_params=pltpu.CompilerParams(vmem_limit_bytes=limit),
        cost_estimate=pl.CostEstimate(flops=flops, bytes_accessed=moved, transcendentals=0),
    )


def iota(shape, dim):
    return lax.broadcasted_iota(jnp.int32, shape, dim)


def pieces(shape, dim=1):
    at = iota(shape, dim)
    piece = jnp.zeros(shape, jnp.int32)
    for i in range(1, PIECES + 1):
        piece = piece + jnp.where(at >= i * CAPACITY, 1, 0)
    return piece, at - piece * CAPACITY


def held_slots(tokens):
    piece, within = pieces((LANES, tokens), 0)
    return jnp.where(piece < PIECES, within, -2).astype(jnp.float32)


def dispatch_kernel(lengths, routes_ref, probs_ref, grad_ref, out_ref, slot_ref):
    width, tokens = grad_ref.shape
    at = iota((1, tokens), 1)
    weight = jnp.zeros((1, tokens), jnp.float32)
    start = jnp.int32(0)
    for i in range(lengths.shape[1]):
        length = lengths[0, i]
        inverse = 1.0 / jnp.full((1, tokens), length, jnp.int32).astype(jnp.float32)
        weight = weight + jnp.where((at >= start) & (at < start + length), inverse, 0.0)
        start = start + length

    label = iota((EXPERTS, tokens), 0)
    hits = jnp.zeros((EXPERTS, tokens), jnp.float32)
    factor = jnp.zeros((EXPERTS, tokens), jnp.float32)
    for k in range(routes_ref.shape[0]):
        named = routes_ref[k : k + 1, :] == label
        hits = hits + jnp.where(named, 1.0, 0.0)
        factor = factor + jnp.where(named, probs_ref[k : k + 1, :] * weight, 0.0)
    above = (iota((tokens, tokens), 0) < iota((tokens, tokens), 1)).astype(jnp.bfloat16)
    before = jnp.dot(hits.astype(jnp.bfloat16), above, preferred_element_type=jnp.float32)
    slot = jnp.where(hits > 0.0, before, -1.0)
    slot_ref[...] = slot

    piece, _ = pieces((1, LANES))
    held = held_slots(tokens)
    chunk = width // PIECES
    source = grad_ref[...].astype(jnp.float32)
    for e in range(EXPERTS):
        pick = jnp.where(slot[e : e + 1, :] == held, 1.0, 0.0).astype(jnp.bfloat16)
        scaled = (source * factor[e : e + 1, :]).astype(jnp.bfloat16)
        full = lax.dot_general(scaled, pick, (((1,), (1,)), ((), ())), preferred_element_type=jnp.float32)
        chosen = full[0:chunk]
        for q in range(1, PIECES):
            chosen = jnp.where(piece == q, full[q * chunk : (q + 1) * chunk], chosen)
        out_ref[e] = chosen.astype(jnp.bfloat16)


def unpack_kernel(in_ref, out_ref):
    shards, chunk, _ = in_ref.shape
    blocks = [in_ref[s].astype(jnp.float32) for s in range(shards)]
    lane = iota((1, LANES), 1)
    for q in range(PIECES):
        turned = [
            pltpu.roll(blocks[s], ((s - q) * CAPACITY) % LANES, 1) if ((s - q) * CAPACITY) % LANES else blocks[s]
            for s in range(shards)
        ]
        for b in range(SLOTS // LANES):
            block = jnp.zeros((chunk, LANES), jnp.float32)
            for s in range(shards):
                low = max(s * CAPACITY - b * LANES, 0)
                high = min((s + 1) * CAPACITY - b * LANES, LANES)
                if low < high:
                    block = jnp.where((lane >= low) & (lane < high), turned[s], block)
            out_ref[q * chunk : (q + 1) * chunk, b * LANES : (b + 1) * LANES] = block.astype(jnp.bfloat16)


def product_kernel(along, place, own_ref, other_ref, *refs):
    weights, out_ref, data = refs[:SIDE], refs[SIDE], refs[SIDE + 1]
    deep = own_ref.shape[1]
    for core in range(CORES):

        @pl.when(place[2] == core)
        def _(core=core):
            both = (own_ref, other_ref) if core == 0 else (other_ref, own_ref)
            for n in range(SIDE):
                data[2 * n * deep : 2 * (n + 1) * deep, :] = jnp.concatenate([ref[n] for ref in both], axis=0)

    for k in range(SIDE):
        part = jnp.dot(weights[k][...], data[...], preferred_element_type=jnp.float32)
        out_ref[lax.rem(place[along] + SIDE - k, SIDE)] = part.astype(jnp.bfloat16)


def added(in_ref):
    total = in_ref[0].astype(jnp.float32)
    for n in range(1, in_ref.shape[0]):
        total = total + in_ref[n].astype(jnp.float32)
    return total


def gate_kernel(in_ref, gate_ref, out_ref):
    out_ref[...] = (added(in_ref) * gate_ref[...].astype(jnp.float32)).astype(jnp.bfloat16)


def pack_kernel(in_ref, out_ref):
    shards, chunk, _ = out_ref.shape
    total = added(in_ref)
    piece, _ = pieces((1, LANES))
    lane = iota((1, LANES), 1)
    for s in range(shards):
        b, low = divmod(s * CAPACITY, LANES)
        block = jnp.zeros((chunk, LANES), jnp.float32)
        for q in range(PIECES):
            rows = total[q * chunk : (q + 1) * chunk]
            part = rows[:, b * LANES : (b + 1) * LANES]
            if low + CAPACITY > LANES:
                part = jnp.where(lane >= low, part, rows[:, (b + 1) * LANES : (b + 2) * LANES])
            turn = (q * CAPACITY - low) % LANES
            block = jnp.where(piece == q, pltpu.roll(part, turn, 1) if turn else part, block)
        out_ref[s] = block.astype(jnp.bfloat16)


def combine_kernel(in_ref, slot_ref, out_ref):
    piece, _ = pieces((1, LANES))
    held = held_slots(slot_ref.shape[1])
    total = jnp.zeros(out_ref.shape, jnp.float32)
    for e in range(in_ref.shape[0]):
        block = in_ref[e].astype(jnp.float32)
        spread = jnp.concatenate([jnp.where(piece == q, block, 0.0) for q in range(PIECES)], axis=0)
        pick = jnp.where(slot_ref[e : e + 1, :] == held, 1.0, 0.0).astype(jnp.bfloat16)
        total = total + jnp.dot(spread.astype(jnp.bfloat16), pick, preferred_element_type=jnp.float32)
    out_ref[...] = total.astype(jnp.bfloat16)


def here():
    me = lax.axis_index("dp")
    return me // (SIDE * CORES), lax.rem(me // CORES, SIDE), lax.rem(me, CORES)


def column_copies(ks, in_ref, out_refs, held, into, out_of):
    wide = in_ref.shape[1] // (SIDE * SIDE)
    taken, given = [], []
    for k in ks:
        for n in range(SIDE):
            block = n * SIDE + lax.rem(here()[1] + k, SIDE)
            columns = pl.ds(pl.multiple_of(block * wide, wide), wide)
            to = held[k].at[:, pl.ds(n * wide, wide)]
            taken.append(pltpu.make_async_copy(in_ref.at[:, columns], to, into.at[len(taken)]))
        given.append(pltpu.make_async_copy(held[k], out_refs[k], out_of.at[k]))
    return taken, given


def first_kernel(lengths, routes_ref, probs_ref, grad_ref, weights, out_ref, slot_ref, *refs):
    parts, held, (into, out_of) = refs[: SIDE - 1], refs[SIDE - 1 : -2], refs[-2:]
    taken, given = column_copies((1, 3, 2), weights, (None, *parts), (None, *held), into, out_of)
    for copy in taken:
        copy.start()
    dispatch_kernel(lengths, routes_ref, probs_ref, grad_ref, out_ref, slot_ref)
    for copy in taken:
        copy.wait()
    for copy in given:
        copy.start()
    for copy in given:
        copy.wait()


def second_kernel(up_ref, down_ref, *refs):
    out_refs, kept_ref, whole, held, kept = refs[:SIDE], refs[SIDE], refs[SIDE + 1], refs[SIDE + 2 : -4], refs[-4]
    fetched, into, out_of = refs[-3:]
    fetch = pltpu.make_async_copy(up_ref, whole, fetched)
    fetch.start()
    taken, given = column_copies((0,), down_ref, (kept_ref,), (kept,), into, out_of)
    for copy in taken:
        copy.start()
    fetch.wait()
    wide = up_ref.shape[1] // SIDE
    for at in range(SIDE):

        @pl.when(here()[0] == at)
        def _(at=at):
            for k in range(SIDE):
                n = (at + k) % SIDE
                held[k][...] = whole[:, n * wide : (n + 1) * wide]

    copies = [pltpu.make_async_copy(held[k], out_refs[k], out_of.at[k + 1]) for k in range(SIDE)]
    for copy in copies:
        copy.start()
    for copy in taken:
        copy.wait()
    for copy in given:
        copy.start()
    for copy in copies + given:
        copy.wait()


def send(part, dx, dy):
    return lax.ppermute(part, "dp", moves(dx, dy))


def product(along, place, rows, weights):
    other = lax.ppermute(rows, "dp", OTHER_CORE)
    _, deep, slots = rows.shape
    return call(
        functools.partial(product_kernel, along),
        jax.ShapeDtypeStruct((SIDE, weights[0].shape[0], slots), jnp.bfloat16),
        1,
        2 + SIDE,
        12 * MIB,
        [pltpu.VMEM((CORES * SIDE * deep, slots), jnp.bfloat16)],
    )(place, rows, other, *weights)


def on_device(grad_out, routes, probs, resp_len, w_down, w_up, gate_act):
    tokens, width = grad_out.shape
    hidden = w_down.shape[1]
    chunk = width // PIECES
    place = jnp.stack(here()).astype(jnp.int32)

    def half(*shape):
        return jax.ShapeDtypeStruct(shape, jnp.bfloat16)

    together = lax.optimization_barrier
    in_smem, in_vmem, in_hbm = (pl.BlockSpec(memory_space=m) for m in (pltpu.SMEM, pltpu.VMEM, pltpu.HBM))
    deep, features = w_down.shape[1:]
    part = half(deep, features // SIDE)
    outgoing, slots, *down = pl.pallas_call(
        first_kernel,
        out_shape=[half(EXPERTS, chunk, LANES), jax.ShapeDtypeStruct((EXPERTS, tokens), jnp.float32)]
        + [part] * (SIDE - 1),
        in_specs=[in_smem] + [in_vmem] * 3 + [in_hbm],
        out_specs=[in_vmem] * 2 + [in_hbm] * (SIDE - 1),
        scratch_shapes=[pltpu.VMEM(part.shape, part.dtype)] * (SIDE - 1)
        + [pltpu.SemaphoreType.DMA(((SIDE - 1) * SIDE,)), pltpu.SemaphoreType.DMA((SIDE,))],
        compiler_params=pltpu.CompilerParams(vmem_limit_bytes=MOST),
    )(resp_len, routes.T, probs.T, grad_out.T, w_down[0])

    arrived = lax.all_to_all(outgoing, "expert", 0, 0, tiled=True)
    up_part = half(width, w_up.shape[2] // SIDE)
    *up, kept = pl.pallas_call(
        second_kernel,
        out_shape=[up_part] * SIDE + [part],
        in_specs=[in_hbm] * 2,
        out_specs=[in_hbm] * (SIDE + 1),
        scratch_shapes=[pltpu.VMEM(w_up.shape[1:], w_up.dtype)]
        + [pltpu.VMEM(up_part.shape, up_part.dtype)] * SIDE
        + [pltpu.VMEM(part.shape, part.dtype)]
        + [pltpu.SemaphoreType.DMA, pltpu.SemaphoreType.DMA((SIDE,)), pltpu.SemaphoreType.DMA((SIDE + 1,))],
        compiler_params=pltpu.CompilerParams(vmem_limit_bytes=MOST),
    )(after(w_up[0], outgoing), w_down[0])
    down = [kept, *down]
    arrived, up = together((arrived, up))
    spread = call(unpack_kernel, half(width, SLOTS), 0, 1)(arrived)
    rows = gather(spread, X_GROUPS)
    rows, *down[1:] = together((rows, *[send(down[k], 0, k) for k in range(1, SIDE)]))
    partial = product(1, place, rows, down)

    partial, up = together((partial, up))
    spread = call(gate_kernel, half(hidden, SLOTS), 0, 2)(exchange(partial, Y_GROUPS), gate_act[0].T)
    rows = gather(spread, Y_GROUPS)
    rows, up[1], up[3], up[2] = together((rows, *[send(up[k], k, 0) for k in (1, 3, 2)]))
    partial = product(0, place, rows, up)
    returning = call(pack_kernel, half(EXPERTS, chunk, LANES), 0, 1)(exchange(partial, X_GROUPS))
    back = lax.all_to_all(returning, "expert", 0, 0, tiled=True)
    return call(combine_kernel, half(width, tokens), 0, 2)(back, slots).T


def solution(mesh):
    in_specs = (
        P("expert", "dp"),
        P("expert", None),
        P("expert", None),
        P("expert", None),
        P("expert", "dp", None),
        P("expert", "dp", None),
        P("expert", None, "dp"),
    )
    out_specs = P("expert", "dp")
    return jax.shard_map(
        on_device, mesh=mesh, in_specs=in_specs, out_specs=out_specs, check_vma=False
    )
```

```python
import functools

import jax
import jax.numpy as jnp
from jax import lax
from jax.experimental import pallas as pl
from jax.experimental.pallas import tpu as pltpu
from jax.sharding import PartitionSpec as P

SIDE = 4
CORES = 2
EXPERTS = 16
CAPACITY = 40
SLOTS = EXPERTS * CAPACITY
LANES = 128
PIECES = LANES // CAPACITY
MIB = 1 << 20
MOST = 58 * MIB


def index(x, y, c):
    return ((x % SIDE) * SIDE + y % SIDE) * CORES + c


X_GROUPS = [[index(x, y, c) for x in range(SIDE)] for y in range(SIDE) for c in range(CORES)]
Y_GROUPS = [[index(x, y, c) for y in range(SIDE)] for x in range(SIDE) for c in range(CORES)]


def moves(dx, dy, swap=0):
    return [
        (index(x, y, c), index(x + dx, y + dy, (c + swap) % CORES))
        for x in range(SIDE)
        for y in range(SIDE)
        for c in range(CORES)
    ]


OTHER_CORE = moves(0, 0, 1)
FIRST = (2, 1, 3)


def exchange(blocks, groups):
    return lax.all_to_all(blocks, "dp", 0, 0, tiled=True, axis_index_groups=groups)


def gather(block, groups):
    return lax.all_gather(block, "dp", axis_index_groups=groups)


def after(value, *others):
    return lax.optimization_barrier((value, *others))[0]


def call(kernel, out_shape, n_scalars, n_arrays, limit=6 * MIB, scratch=(), flops=0, moved=0):
    return pl.pallas_call(
        kernel,
        out_shape=out_shape,
        in_specs=[pl.BlockSpec(memory_space=pltpu.SMEM)] * n_scalars
        + [pl.BlockSpec(memory_space=pltpu.VMEM)] * n_arrays,
        out_specs=jax.tree.map(lambda _: pl.BlockSpec(memory_space=pltpu.VMEM), out_shape),
        scratch_shapes=scratch,
        compiler_params=pltpu.CompilerParams(vmem_limit_bytes=limit),
        cost_estimate=pl.CostEstimate(flops=flops, bytes_accessed=moved, transcendentals=0),
    )


def iota(shape, dim):
    return lax.broadcasted_iota(jnp.int32, shape, dim)


def pieces(shape, dim=1):
    at = iota(shape, dim)
    piece = jnp.zeros(shape, jnp.int32)
    for i in range(1, PIECES + 1):
        piece = piece + jnp.where(at >= i * CAPACITY, 1, 0)
    return piece, at - piece * CAPACITY


def held_slots(tokens):
    piece, within = pieces((LANES, tokens), 0)
    return jnp.where(piece < PIECES, within, -2).astype(jnp.float32)


def dispatch_kernel(lengths, routes_ref, probs_ref, grad_ref, out_ref, slot_ref, at_expert):
    width, tokens = grad_ref.shape
    at = iota((1, tokens), 1)
    weight = jnp.zeros((1, tokens), jnp.float32)
    start = jnp.int32(0)
    for i in range(lengths.shape[1]):
        length = lengths[0, i]
        inverse = 1.0 / jnp.full((1, tokens), length, jnp.int32).astype(jnp.float32)
        weight = weight + jnp.where((at >= start) & (at < start + length), inverse, 0.0)
        start = start + length

    label = iota((EXPERTS, tokens), 0)
    hits = jnp.zeros((EXPERTS, tokens), jnp.float32)
    factor = jnp.zeros((EXPERTS, tokens), jnp.float32)
    for k in range(routes_ref.shape[0]):
        named = routes_ref[k : k + 1, :] == label
        hits = hits + jnp.where(named, 1.0, 0.0)
        factor = factor + jnp.where(named, probs_ref[k : k + 1, :] * weight, 0.0)
    above = (iota((tokens, tokens), 0) < iota((tokens, tokens), 1)).astype(jnp.bfloat16)
    before = jnp.dot(hits.astype(jnp.bfloat16), above, preferred_element_type=jnp.float32)
    slot = jnp.where(hits > 0.0, before, -1.0)
    slot_ref[...] = slot

    piece, _ = pieces((1, LANES))
    held = held_slots(tokens)
    chunk = width // PIECES
    source = grad_ref[...].astype(jnp.float32)
    for e in range(EXPERTS):
        at_expert(e)
        pick = jnp.where(slot[e : e + 1, :] == held, 1.0, 0.0).astype(jnp.bfloat16)
        scaled = (source * factor[e : e + 1, :]).astype(jnp.bfloat16)
        full = lax.dot_general(scaled, pick, (((1,), (1,)), ((), ())), preferred_element_type=jnp.float32)
        chosen = full[0:chunk]
        for q in range(1, PIECES):
            chosen = jnp.where(piece == q, full[q * chunk : (q + 1) * chunk], chosen)
        out_ref[e] = chosen.astype(jnp.bfloat16)


def unpack_kernel(in_ref, out_ref):
    shards, chunk, _ = in_ref.shape
    blocks = [in_ref[s].astype(jnp.float32) for s in range(shards)]
    lane = iota((1, LANES), 1)
    for q in range(PIECES):
        turned = [
            pltpu.roll(blocks[s], ((s - q) * CAPACITY) % LANES, 1) if ((s - q) * CAPACITY) % LANES else blocks[s]
            for s in range(shards)
        ]
        for b in range(SLOTS // LANES):
            block = jnp.zeros((chunk, LANES), jnp.float32)
            for s in range(shards):
                low = max(s * CAPACITY - b * LANES, 0)
                high = min((s + 1) * CAPACITY - b * LANES, LANES)
                if low < high:
                    block = jnp.where((lane >= low) & (lane < high), turned[s], block)
            out_ref[q * chunk : (q + 1) * chunk, b * LANES : (b + 1) * LANES] = block.astype(jnp.bfloat16)


def product_kernel(along, place, own_ref, other_ref, *refs):
    weights, out_ref, data = refs[:SIDE], refs[SIDE], refs[SIDE + 1]
    deep = own_ref.shape[1]
    for core in range(CORES):

        @pl.when(place[2] == core)
        def _(core=core):
            both = (own_ref, other_ref) if core == 0 else (other_ref, own_ref)
            for n in range(SIDE):
                data[2 * n * deep : 2 * (n + 1) * deep, :] = jnp.concatenate([ref[n] for ref in both], axis=0)

    for k in range(SIDE):
        part = jnp.dot(weights[k][...], data[...], preferred_element_type=jnp.float32)
        out_ref[lax.rem(place[along] + SIDE - k, SIDE)] = part.astype(jnp.bfloat16)


def added(in_ref):
    total = in_ref[0].astype(jnp.float32)
    for n in range(1, in_ref.shape[0]):
        total = total + in_ref[n].astype(jnp.float32)
    return total


def gate_kernel(in_ref, gate_ref, out_ref):
    out_ref[...] = (added(in_ref) * gate_ref[...].astype(jnp.float32)).astype(jnp.bfloat16)


def pack_kernel(in_ref, out_ref):
    shards, chunk, _ = out_ref.shape
    total = added(in_ref)
    piece, _ = pieces((1, LANES))
    lane = iota((1, LANES), 1)
    for s in range(shards):
        b, low = divmod(s * CAPACITY, LANES)
        block = jnp.zeros((chunk, LANES), jnp.float32)
        for q in range(PIECES):
            rows = total[q * chunk : (q + 1) * chunk]
            part = rows[:, b * LANES : (b + 1) * LANES]
            if low + CAPACITY > LANES:
                part = jnp.where(lane >= low, part, rows[:, (b + 1) * LANES : (b + 2) * LANES])
            turn = (q * CAPACITY - low) % LANES
            block = jnp.where(piece == q, pltpu.roll(part, turn, 1) if turn else part, block)
        out_ref[s] = block.astype(jnp.bfloat16)


def combine_kernel(in_ref, slot_ref, out_ref):
    piece, _ = pieces((1, LANES))
    held = held_slots(slot_ref.shape[1])
    total = jnp.zeros(out_ref.shape, jnp.float32)
    for e in range(in_ref.shape[0]):
        block = in_ref[e].astype(jnp.float32)
        spread = jnp.concatenate([jnp.where(piece == q, block, 0.0) for q in range(PIECES)], axis=0)
        pick = jnp.where(slot_ref[e : e + 1, :] == held, 1.0, 0.0).astype(jnp.bfloat16)
        total = total + jnp.dot(spread.astype(jnp.bfloat16), pick, preferred_element_type=jnp.float32)
    out_ref[...] = total.astype(jnp.bfloat16)


def here():
    me = lax.axis_index("dp")
    return me // (SIDE * CORES), lax.rem(me // CORES, SIDE), lax.rem(me, CORES)


def column_copies(ks, in_ref, held, sems):
    wide = in_ref.shape[1] // (SIDE * SIDE)
    copies = []
    for to, k in zip(held, ks):
        for n in range(SIDE):
            block = n * SIDE + lax.rem(here()[1] + k, SIDE)
            columns = pl.ds(pl.multiple_of(block * wide, wide), wide)
            sem = sems.at[len(copies)]
            copies.append(pltpu.make_async_copy(in_ref.at[:, columns], to.at[:, pl.ds(n * wide, wide)], sem))
    return copies


def first_kernel(lengths, routes_ref, probs_ref, grad_ref, weights, out_ref, slot_ref, *refs):
    parts, held, (into, out_of) = refs[: SIDE - 1], refs[SIDE - 1 : -2], refs[-2:]
    taken = column_copies(FIRST, weights, held, into)
    given = [pltpu.make_async_copy(held[i], parts[i], out_of.at[i]) for i in range(SIDE - 1)]
    for copy in taken:
        copy.start()

    def pass_on(expert):
        i = expert // SIDE - 1
        if expert % SIDE == 0 and i >= 0:
            for copy in taken[i * SIDE : (i + 1) * SIDE]:
                copy.wait()
            given[i].start()

    dispatch_kernel(lengths, routes_ref, probs_ref, grad_ref, out_ref, slot_ref, pass_on)
    for copy in given:
        copy.wait()


def cut_up_kernel(up_ref, down_ref, *refs):
    out_refs, (kept_ref, windows, held, kept, fetched, out_of, into, kept_out) = refs[:SIDE], refs[SIDE:]
    wide, window = held.shape[2], windows.shape[2]
    fetches = []
    for n in range(SIDE):
        columns = pl.ds(n * wide // LANES * LANES, window)
        fetches.append(pltpu.make_async_copy(up_ref.at[:, columns], windows.at[n], fetched.at[n]))
    taken = column_copies((0,), down_ref, (kept,), into)
    for copy in fetches + taken:
        copy.start()
    given = [[pltpu.make_async_copy(held.at[n], ref, out_of.at[n]) for ref in out_refs] for n in range(SIDE)]

    def given_on(n, act):
        for k in range(SIDE):

            @pl.when(lax.rem(here()[0] + k, SIDE) == n)
            def _(k=k):
                act(given[n][k])

    for n in range(SIDE):
        fetches[n].wait()
        skip = n * wide % LANES
        held[n] = windows[n, :, skip : skip + wide]
        given_on(n, lambda copy: copy.start())
    for copy in taken:
        copy.wait()
    last = pltpu.make_async_copy(kept, kept_ref, kept_out)
    last.start()
    for n in range(SIDE):
        given_on(n, lambda copy: copy.wait())
    last.wait()


def send(part, dx, dy):
    return lax.ppermute(part, "dp", moves(dx, dy))


def product(along, place, rows, other, weights):
    _, deep, slots = rows.shape
    return call(
        functools.partial(product_kernel, along),
        jax.ShapeDtypeStruct((SIDE, weights[0].shape[0], slots), jnp.bfloat16),
        1,
        2 + SIDE,
        12 * MIB,
        [pltpu.VMEM((CORES * SIDE * deep, slots), jnp.bfloat16)],
    )(place, rows, other, *weights)


def on_device(grad_out, routes, probs, resp_len, w_down, w_up, gate_act):
    tokens, width = grad_out.shape
    hidden = w_down.shape[1]
    chunk = width // PIECES
    place = jnp.stack(here()).astype(jnp.int32)

    def half(*shape):
        return jax.ShapeDtypeStruct(shape, jnp.bfloat16)

    together = lax.optimization_barrier
    in_smem, in_vmem, in_hbm = (pl.BlockSpec(memory_space=m) for m in (pltpu.SMEM, pltpu.VMEM, pltpu.HBM))
    deep, features = w_down.shape[1:]
    part = half(deep, features // SIDE)
    outgoing, slots, *down = pl.pallas_call(
        first_kernel,
        out_shape=[half(EXPERTS, chunk, LANES), jax.ShapeDtypeStruct((EXPERTS, tokens), jnp.float32)]
        + [part] * (SIDE - 1),
        in_specs=[in_smem] + [in_vmem] * 3 + [in_hbm],
        out_specs=[in_vmem] * 2 + [in_hbm] * (SIDE - 1),
        scratch_shapes=[pltpu.VMEM(part.shape, part.dtype)] * (SIDE - 1)
        + [pltpu.SemaphoreType.DMA(((SIDE - 1) * SIDE,)), pltpu.SemaphoreType.DMA((SIDE - 1,))],
        compiler_params=pltpu.CompilerParams(vmem_limit_bytes=MOST),
    )(resp_len, routes.T, probs.T, grad_out.T, w_down[0])

    arrived = lax.all_to_all(outgoing, "expert", 0, 0, tiled=True)
    spread = call(unpack_kernel, half(width, SLOTS), 0, 1)(arrived)
    rows = gather(spread, X_GROUPS)
    rows, *down = together((rows, *[send(cut, 0, k) for k, cut in zip(FIRST, down)]))

    up_part = half(width, w_up.shape[2] // SIDE)
    window = -(-(up_part.shape[1] + LANES // 2) // LANES) * LANES
    *up, kept = pl.pallas_call(
        cut_up_kernel,
        out_shape=[up_part] * SIDE + [part],
        in_specs=[in_hbm] * 2,
        out_specs=[in_hbm] * (SIDE + 1),
        scratch_shapes=[
            pltpu.VMEM((SIDE, width, window), w_up.dtype),
            pltpu.VMEM((SIDE, *up_part.shape), w_up.dtype),
            pltpu.VMEM(part.shape, part.dtype),
        ]
        + [pltpu.SemaphoreType.DMA((SIDE,))] * 3
        + [pltpu.SemaphoreType.DMA],
        compiler_params=pltpu.CompilerParams(vmem_limit_bytes=MOST),
    )(after(w_up[0], rows), w_down[0])
    down = dict(zip(FIRST, down))
    partial = product(1, place, rows, lax.ppermute(rows, "dp", OTHER_CORE), [kept, *[down[k] for k in range(1, SIDE)]])

    partial, up = together((partial, up))
    spread = call(gate_kernel, half(hidden, SLOTS), 0, 2)(exchange(partial, Y_GROUPS), gate_act[0].T)
    rows = gather(spread, Y_GROUPS)
    rows, *sent = together((rows, *[send(up[k], k, 0) for k in FIRST]))
    up = [up[0]] + [sent[FIRST.index(k)] for k in range(1, SIDE)]
    partial = product(0, place, rows, lax.ppermute(rows, "dp", OTHER_CORE), up)
    returning = call(pack_kernel, half(EXPERTS, chunk, LANES), 0, 1)(exchange(partial, X_GROUPS))
    back = lax.all_to_all(returning, "expert", 0, 0, tiled=True)
    return call(combine_kernel, half(width, tokens), 0, 2)(back, slots).T


def solution(mesh):
    in_specs = (
        P("expert", "dp"),
        P("expert", None),
        P("expert", None),
        P("expert", None),
        P("expert", "dp", None),
        P("expert", "dp", None),
        P("expert", None, "dp"),
    )
    out_specs = P("expert", "dp")
    return jax.shard_map(
        on_device, mesh=mesh, in_specs=in_specs, out_specs=out_specs, check_vma=False
    )
```

```python
import functools

import jax
import jax.numpy as jnp
from jax import lax
from jax.experimental import pallas as pl
from jax.experimental.pallas import tpu as pltpu
from jax.sharding import PartitionSpec as P

SIDE = 4
CORES = 2
EXPERTS = 16
CAPACITY = 40
SLOTS = EXPERTS * CAPACITY
LANES = 128
PIECES = LANES // CAPACITY
MIB = 1 << 20
MOST = 58 * MIB


def index(x, y, c):
    return ((x % SIDE) * SIDE + y % SIDE) * CORES + c


X_GROUPS = [[index(x, y, c) for x in range(SIDE)] for y in range(SIDE) for c in range(CORES)]
Y_GROUPS = [[index(x, y, c) for y in range(SIDE)] for x in range(SIDE) for c in range(CORES)]


def moves(dx, dy, swap=0):
    return [
        (index(x, y, c), index(x + dx, y + dy, (c + swap) % CORES))
        for x in range(SIDE)
        for y in range(SIDE)
        for c in range(CORES)
    ]


OTHER_CORE = moves(0, 0, 1)
FIRST = (2, 1, 3)


def exchange(blocks, groups):
    return lax.all_to_all(blocks, "dp", 0, 0, tiled=True, axis_index_groups=groups)


def gather(block, groups):
    return lax.all_gather(block, "dp", axis_index_groups=groups)


def after(value, *others):
    return lax.optimization_barrier((value, *others))[0]


def call(kernel, out_shape, n_scalars, n_arrays, limit=6 * MIB, scratch=(), flops=0, moved=0):
    return pl.pallas_call(
        kernel,
        out_shape=out_shape,
        in_specs=[pl.BlockSpec(memory_space=pltpu.SMEM)] * n_scalars
        + [pl.BlockSpec(memory_space=pltpu.VMEM)] * n_arrays,
        out_specs=jax.tree.map(lambda _: pl.BlockSpec(memory_space=pltpu.VMEM), out_shape),
        scratch_shapes=scratch,
        compiler_params=pltpu.CompilerParams(vmem_limit_bytes=limit),
        cost_estimate=pl.CostEstimate(flops=flops, bytes_accessed=moved, transcendentals=0),
    )


def iota(shape, dim):
    return lax.broadcasted_iota(jnp.int32, shape, dim)


def pieces(shape, dim=1):
    at = iota(shape, dim)
    piece = jnp.zeros(shape, jnp.int32)
    for i in range(1, PIECES + 1):
        piece = piece + jnp.where(at >= i * CAPACITY, 1, 0)
    return piece, at - piece * CAPACITY


def held_slots(tokens):
    piece, within = pieces((LANES, tokens), 0)
    return jnp.where(piece < PIECES, within, -2).astype(jnp.float32)


def dispatch_kernel(lengths, routes_ref, probs_ref, grad_ref, out_ref, slot_ref, at_expert):
    width, tokens = grad_ref.shape
    at = iota((1, tokens), 1)
    weight = jnp.zeros((1, tokens), jnp.float32)
    start = jnp.int32(0)
    for i in range(lengths.shape[1]):
        length = lengths[0, i]
        inverse = 1.0 / jnp.full((1, tokens), length, jnp.int32).astype(jnp.float32)
        weight = weight + jnp.where((at >= start) & (at < start + length), inverse, 0.0)
        start = start + length

    label = iota((EXPERTS, tokens), 0)
    hits = jnp.zeros((EXPERTS, tokens), jnp.float32)
    factor = jnp.zeros((EXPERTS, tokens), jnp.float32)
    for k in range(routes_ref.shape[0]):
        named = routes_ref[k : k + 1, :] == label
        hits = hits + jnp.where(named, 1.0, 0.0)
        factor = factor + jnp.where(named, probs_ref[k : k + 1, :] * weight, 0.0)
    above = (iota((tokens, tokens), 0) < iota((tokens, tokens), 1)).astype(jnp.bfloat16)
    before = jnp.dot(hits.astype(jnp.bfloat16), above, preferred_element_type=jnp.float32)
    slot = jnp.where(hits > 0.0, before, -1.0)
    slot_ref[...] = slot

    piece, _ = pieces((1, LANES))
    held = held_slots(tokens)
    chunk = width // PIECES
    source = grad_ref[...].astype(jnp.float32)
    for e in range(EXPERTS):
        at_expert(e)
        pick = jnp.where(slot[e : e + 1, :] == held, 1.0, 0.0).astype(jnp.bfloat16)
        scaled = (source * factor[e : e + 1, :]).astype(jnp.bfloat16)
        full = lax.dot_general(scaled, pick, (((1,), (1,)), ((), ())), preferred_element_type=jnp.float32)
        chosen = full[0:chunk]
        for q in range(1, PIECES):
            chosen = jnp.where(piece == q, full[q * chunk : (q + 1) * chunk], chosen)
        out_ref[e] = chosen.astype(jnp.bfloat16)


def unpack_kernel(in_ref, out_ref):
    shards, chunk, _ = in_ref.shape
    blocks = [in_ref[s].astype(jnp.float32) for s in range(shards)]
    lane = iota((1, LANES), 1)
    for q in range(PIECES):
        turned = [
            pltpu.roll(blocks[s], ((s - q) * CAPACITY) % LANES, 1) if ((s - q) * CAPACITY) % LANES else blocks[s]
            for s in range(shards)
        ]
        for b in range(SLOTS // LANES):
            block = jnp.zeros((chunk, LANES), jnp.float32)
            for s in range(shards):
                low = max(s * CAPACITY - b * LANES, 0)
                high = min((s + 1) * CAPACITY - b * LANES, LANES)
                if low < high:
                    block = jnp.where((lane >= low) & (lane < high), turned[s], block)
            out_ref[q * chunk : (q + 1) * chunk, b * LANES : (b + 1) * LANES] = block.astype(jnp.bfloat16)


def product_kernel(along, place, own_ref, other_ref, *refs):
    weights, out_ref, data = refs[:SIDE], refs[SIDE], refs[SIDE + 1]
    deep = own_ref.shape[1]
    for core in range(CORES):

        @pl.when(place[2] == core)
        def _(core=core):
            both = (own_ref, other_ref) if core == 0 else (other_ref, own_ref)
            for n in range(SIDE):
                data[2 * n * deep : 2 * (n + 1) * deep, :] = jnp.concatenate([ref[n] for ref in both], axis=0)

    for k in range(SIDE):
        part = jnp.dot(weights[k][...], data[...], preferred_element_type=jnp.float32)
        out_ref[lax.rem(place[along] + SIDE - k, SIDE)] = part.astype(jnp.bfloat16)


def part_kernel(weights, data_ref, out_ref):
    out_ref[...] = jnp.dot(weights[...], data_ref[...], preferred_element_type=jnp.float32).astype(jnp.bfloat16)


def first_part_kernel(place, own_ref, other_ref, weights, data_ref, out_ref):
    deep = own_ref.shape[1]
    for core in range(CORES):

        @pl.when(place[2] == core)
        def _(core=core):
            both = (own_ref, other_ref) if core == 0 else (other_ref, own_ref)
            for n in range(SIDE):
                data_ref[2 * n * deep : 2 * (n + 1) * deep, :] = jnp.concatenate([ref[n] for ref in both], axis=0)

    part_kernel(weights, data_ref, out_ref)


def added(in_ref):
    total = in_ref[0].astype(jnp.float32)
    for n in range(1, in_ref.shape[0]):
        total = total + in_ref[n].astype(jnp.float32)
    return total


def gate_kernel(in_ref, gate_ref, out_ref):
    out_ref[...] = (added(in_ref) * gate_ref[...].astype(jnp.float32)).astype(jnp.bfloat16)


def pack_kernel(*refs):
    in_refs, out_ref = refs[:-1], refs[-1]
    shards, chunk, _ = out_ref.shape
    total = in_refs[0][...].astype(jnp.float32)
    for ref in in_refs[1:]:
        total = total + ref[...].astype(jnp.float32)
    piece, _ = pieces((1, LANES))
    lane = iota((1, LANES), 1)
    for s in range(shards):
        b, low = divmod(s * CAPACITY, LANES)
        block = jnp.zeros((chunk, LANES), jnp.float32)
        for q in range(PIECES):
            rows = total[q * chunk : (q + 1) * chunk]
            part = rows[:, b * LANES : (b + 1) * LANES]
            if low + CAPACITY > LANES:
                part = jnp.where(lane >= low, part, rows[:, (b + 1) * LANES : (b + 2) * LANES])
            turn = (q * CAPACITY - low) % LANES
            block = jnp.where(piece == q, pltpu.roll(part, turn, 1) if turn else part, block)
        out_ref[s] = block.astype(jnp.bfloat16)


def combine_kernel(in_ref, slot_ref, out_ref):
    piece, _ = pieces((1, LANES))
    held = held_slots(slot_ref.shape[1])
    total = jnp.zeros(out_ref.shape, jnp.float32)
    for e in range(in_ref.shape[0]):
        block = in_ref[e].astype(jnp.float32)
        spread = jnp.concatenate([jnp.where(piece == q, block, 0.0) for q in range(PIECES)], axis=0)
        pick = jnp.where(slot_ref[e : e + 1, :] == held, 1.0, 0.0).astype(jnp.bfloat16)
        total = total + jnp.dot(spread.astype(jnp.bfloat16), pick, preferred_element_type=jnp.float32)
    out_ref[...] = total.astype(jnp.bfloat16)


def here():
    me = lax.axis_index("dp")
    return me // (SIDE * CORES), lax.rem(me // CORES, SIDE), lax.rem(me, CORES)


def column_copies(ks, in_ref, held, sems):
    wide = in_ref.shape[1] // (SIDE * SIDE)
    copies = []
    for to, k in zip(held, ks):
        for n in range(SIDE):
            block = n * SIDE + lax.rem(here()[1] + k, SIDE)
            columns = pl.ds(pl.multiple_of(block * wide, wide), wide)
            sem = sems.at[len(copies)]
            copies.append(pltpu.make_async_copy(in_ref.at[:, columns], to.at[:, pl.ds(n * wide, wide)], sem))
    return copies


def first_kernel(lengths, routes_ref, probs_ref, grad_ref, weights, out_ref, slot_ref, *refs):
    parts, held, (into, out_of) = refs[: SIDE - 1], refs[SIDE - 1 : -2], refs[-2:]
    taken = column_copies(FIRST, weights, held, into)
    given = [pltpu.make_async_copy(held[i], parts[i], out_of.at[i]) for i in range(SIDE - 1)]
    for copy in taken:
        copy.start()

    def pass_on(expert):
        i = expert // SIDE - 1
        if expert % SIDE == 0 and i >= 0:
            for copy in taken[i * SIDE : (i + 1) * SIDE]:
                copy.wait()
            given[i].start()

    dispatch_kernel(lengths, routes_ref, probs_ref, grad_ref, out_ref, slot_ref, pass_on)
    for copy in given:
        copy.wait()


def cut_up_kernel(up_ref, down_ref, *refs):
    out_refs, (kept_ref, windows, held, kept, fetched, out_of, into, kept_out) = refs[:SIDE], refs[SIDE:]
    wide, window = held.shape[2], windows.shape[2]
    fetches = []
    for n in range(SIDE):
        columns = pl.ds(n * wide // LANES * LANES, window)
        fetches.append(pltpu.make_async_copy(up_ref.at[:, columns], windows.at[n], fetched.at[n]))
    taken = column_copies((0,), down_ref, (kept,), into)
    for copy in fetches + taken:
        copy.start()
    given = [[pltpu.make_async_copy(held.at[n], ref, out_of.at[n]) for ref in out_refs] for n in range(SIDE)]

    def given_on(n, act):
        for k in range(SIDE):

            @pl.when(lax.rem(here()[0] + k, SIDE) == n)
            def _(k=k):
                act(given[n][k])

    for n in range(SIDE):
        fetches[n].wait()
        skip = n * wide % LANES
        held[n] = windows[n, :, skip : skip + wide]
        given_on(n, lambda copy: copy.start())
    for copy in taken:
        copy.wait()
    last = pltpu.make_async_copy(kept, kept_ref, kept_out)
    last.start()
    for n in range(SIDE):
        given_on(n, lambda copy: copy.wait())
    last.wait()


def send(part, dx, dy):
    return lax.ppermute(part, "dp", moves(dx, dy))


def product(along, place, rows, other, weights):
    _, deep, slots = rows.shape
    return call(
        functools.partial(product_kernel, along),
        jax.ShapeDtypeStruct((SIDE, weights[0].shape[0], slots), jnp.bfloat16),
        1,
        2 + SIDE,
        12 * MIB,
        [pltpu.VMEM((CORES * SIDE * deep, slots), jnp.bfloat16)],
    )(place, rows, other, *weights)


def on_device(grad_out, routes, probs, resp_len, w_down, w_up, gate_act):
    tokens, width = grad_out.shape
    hidden = w_down.shape[1]
    chunk = width // PIECES
    place = jnp.stack(here()).astype(jnp.int32)

    def half(*shape):
        return jax.ShapeDtypeStruct(shape, jnp.bfloat16)

    together = lax.optimization_barrier
    in_smem, in_vmem, in_hbm = (pl.BlockSpec(memory_space=m) for m in (pltpu.SMEM, pltpu.VMEM, pltpu.HBM))
    deep, features = w_down.shape[1:]
    part = half(deep, features // SIDE)
    outgoing, slots, *down = pl.pallas_call(
        first_kernel,
        out_shape=[half(EXPERTS, chunk, LANES), jax.ShapeDtypeStruct((EXPERTS, tokens), jnp.float32)]
        + [part] * (SIDE - 1),
        in_specs=[in_smem] + [in_vmem] * 3 + [in_hbm],
        out_specs=[in_vmem] * 2 + [in_hbm] * (SIDE - 1),
        scratch_shapes=[pltpu.VMEM(part.shape, part.dtype)] * (SIDE - 1)
        + [pltpu.SemaphoreType.DMA(((SIDE - 1) * SIDE,)), pltpu.SemaphoreType.DMA((SIDE - 1,))],
        compiler_params=pltpu.CompilerParams(vmem_limit_bytes=MOST),
    )(resp_len, routes.T, probs.T, grad_out.T, w_down[0])

    arrived = lax.all_to_all(outgoing, "expert", 0, 0, tiled=True)
    spread = call(unpack_kernel, half(width, SLOTS), 0, 1)(arrived)
    rows = gather(spread, X_GROUPS)
    rows, *down = together((rows, *[send(cut, 0, k) for k, cut in zip(FIRST, down)]))

    up_part = half(width, w_up.shape[2] // SIDE)
    window = -(-(up_part.shape[1] + LANES // 2) // LANES) * LANES
    *up, kept = pl.pallas_call(
        cut_up_kernel,
        out_shape=[up_part] * SIDE + [part],
        in_specs=[in_hbm] * 2,
        out_specs=[in_hbm] * (SIDE + 1),
        scratch_shapes=[
            pltpu.VMEM((SIDE, width, window), w_up.dtype),
            pltpu.VMEM((SIDE, *up_part.shape), w_up.dtype),
            pltpu.VMEM(part.shape, part.dtype),
        ]
        + [pltpu.SemaphoreType.DMA((SIDE,))] * 3
        + [pltpu.SemaphoreType.DMA],
        compiler_params=pltpu.CompilerParams(vmem_limit_bytes=MOST),
    )(after(w_up[0], rows), w_down[0])
    down = dict(zip(FIRST, down))
    partial = product(1, place, rows, lax.ppermute(rows, "dp", OTHER_CORE), [kept, *[down[k] for k in range(1, SIDE)]])

    partial, up = together((partial, up))
    spread = call(gate_kernel, half(hidden, SLOTS), 0, 2)(exchange(partial, Y_GROUPS), gate_act[0].T)
    rows = gather(spread, Y_GROUPS)
    rows, *sent = together((rows, *[send(up[k], k, 0) for k in FIRST]))
    up = [up[0]] + [sent[FIRST.index(k)] for k in range(1, SIDE)]
    other = lax.ppermute(rows, "dp", OTHER_CORE)
    depth = CORES * SIDE * hidden
    cost = dict(flops=2 * width * depth * SLOTS, moved=2 * depth * (width + SLOTS))
    data, part_sent = call(first_part_kernel, [half(depth, SLOTS), half(width, SLOTS)], 1, 3, **cost)(
        place, rows, other, up[FIRST[0]]
    )
    sums = [send(part_sent, -FIRST[0], 0)]
    for k in (*FIRST[1:], 0):
        done = call(part_kernel, half(width, SLOTS), 0, 2, **cost)(up[k], data)
        sums.append(send(done, -k, 0) if k else done)
    returning = call(pack_kernel, half(EXPERTS, chunk, LANES), 0, SIDE)(*sums)
    back = lax.all_to_all(returning, "expert", 0, 0, tiled=True)
    return call(combine_kernel, half(width, tokens), 0, 2)(back, slots).T


def solution(mesh):
    in_specs = (
        P("expert", "dp"),
        P("expert", None),
        P("expert", None),
        P("expert", None),
        P("expert", "dp", None),
        P("expert", "dp", None),
        P("expert", None, "dp"),
    )
    out_specs = P("expert", "dp")
    return jax.shard_map(
        on_device, mesh=mesh, in_specs=in_specs, out_specs=out_specs, check_vma=False
    )
```

```python
import functools

import jax
import jax.numpy as jnp
from jax import lax
from jax.experimental import pallas as pl
from jax.experimental.pallas import tpu as pltpu
from jax.sharding import PartitionSpec as P

SIDE = 4
CORES = 2
EXPERTS = 16
CAPACITY = 40
SLOTS = EXPERTS * CAPACITY
LANES = 128
PIECES = LANES // CAPACITY
MIB = 1 << 20
MOST = 58 * MIB


def index(x, y, c):
    return ((x % SIDE) * SIDE + y % SIDE) * CORES + c


X_GROUPS = [[index(x, y, c) for x in range(SIDE)] for y in range(SIDE) for c in range(CORES)]
Y_GROUPS = [[index(x, y, c) for y in range(SIDE)] for x in range(SIDE) for c in range(CORES)]


def moves(dx, dy, swap=0):
    return [
        (index(x, y, c), index(x + dx, y + dy, (c + swap) % CORES))
        for x in range(SIDE)
        for y in range(SIDE)
        for c in range(CORES)
    ]


OTHER_CORE = moves(0, 0, 1)
FIRST = (2, 1, 3)


def exchange(blocks, groups):
    return lax.all_to_all(blocks, "dp", 0, 0, tiled=True, axis_index_groups=groups)


def gather(block, groups):
    return lax.all_gather(block, "dp", axis_index_groups=groups)


def after(value, *others):
    return lax.optimization_barrier((value, *others))[0]


def call(kernel, out_shape, n_scalars, n_arrays, limit=6 * MIB, scratch=(), flops=0, moved=0):
    return pl.pallas_call(
        kernel,
        out_shape=out_shape,
        in_specs=[pl.BlockSpec(memory_space=pltpu.SMEM)] * n_scalars
        + [pl.BlockSpec(memory_space=pltpu.VMEM)] * n_arrays,
        out_specs=jax.tree.map(lambda _: pl.BlockSpec(memory_space=pltpu.VMEM), out_shape),
        scratch_shapes=scratch,
        compiler_params=pltpu.CompilerParams(vmem_limit_bytes=limit),
        cost_estimate=pl.CostEstimate(flops=flops, bytes_accessed=moved, transcendentals=0),
    )


def iota(shape, dim):
    return lax.broadcasted_iota(jnp.int32, shape, dim)


def pieces(shape, dim=1):
    at = iota(shape, dim)
    piece = jnp.zeros(shape, jnp.int32)
    for i in range(1, PIECES + 1):
        piece = piece + jnp.where(at >= i * CAPACITY, 1, 0)
    return piece, at - piece * CAPACITY


def held_slots(tokens):
    piece, within = pieces((LANES, tokens), 0)
    return jnp.where(piece < PIECES, within, -2).astype(jnp.float32)


def dispatch_kernel(lengths, routes_ref, probs_ref, grad_ref, out_ref, slot_ref, at_expert):
    width, tokens = grad_ref.shape
    at = iota((1, tokens), 1)
    weight = jnp.zeros((1, tokens), jnp.float32)
    start = jnp.int32(0)
    for i in range(lengths.shape[1]):
        length = lengths[0, i]
        inverse = 1.0 / jnp.full((1, tokens), length, jnp.int32).astype(jnp.float32)
        weight = weight + jnp.where((at >= start) & (at < start + length), inverse, 0.0)
        start = start + length

    label = iota((EXPERTS, tokens), 0)
    hits = jnp.zeros((EXPERTS, tokens), jnp.float32)
    factor = jnp.zeros((EXPERTS, tokens), jnp.float32)
    for k in range(routes_ref.shape[0]):
        named = routes_ref[k : k + 1, :] == label
        hits = hits + jnp.where(named, 1.0, 0.0)
        factor = factor + jnp.where(named, probs_ref[k : k + 1, :] * weight, 0.0)
    above = (iota((tokens, tokens), 0) < iota((tokens, tokens), 1)).astype(jnp.bfloat16)
    before = jnp.dot(hits.astype(jnp.bfloat16), above, preferred_element_type=jnp.float32)
    slot = jnp.where(hits > 0.0, before, -1.0)
    slot_ref[...] = slot

    piece, _ = pieces((1, LANES))
    held = held_slots(tokens)
    chunk = width // PIECES
    source = grad_ref[...].astype(jnp.float32)
    for e in range(EXPERTS):
        at_expert(e)
        pick = jnp.where(slot[e : e + 1, :] == held, 1.0, 0.0).astype(jnp.bfloat16)
        scaled = (source * factor[e : e + 1, :]).astype(jnp.bfloat16)
        full = lax.dot_general(scaled, pick, (((1,), (1,)), ((), ())), preferred_element_type=jnp.float32)
        chosen = full[0:chunk]
        for q in range(1, PIECES):
            chosen = jnp.where(piece == q, full[q * chunk : (q + 1) * chunk], chosen)
        out_ref[e] = chosen.astype(jnp.bfloat16)


def unpack_kernel(in_ref, out_ref):
    shards, chunk, _ = in_ref.shape
    blocks = [in_ref[s].astype(jnp.float32) for s in range(shards)]
    lane = iota((1, LANES), 1)
    for q in range(PIECES):
        turned = [
            pltpu.roll(blocks[s], ((s - q) * CAPACITY) % LANES, 1) if ((s - q) * CAPACITY) % LANES else blocks[s]
            for s in range(shards)
        ]
        for b in range(SLOTS // LANES):
            block = jnp.zeros((chunk, LANES), jnp.float32)
            for s in range(shards):
                low = max(s * CAPACITY - b * LANES, 0)
                high = min((s + 1) * CAPACITY - b * LANES, LANES)
                if low < high:
                    block = jnp.where((lane >= low) & (lane < high), turned[s], block)
            out_ref[q * chunk : (q + 1) * chunk, b * LANES : (b + 1) * LANES] = block.astype(jnp.bfloat16)


def product_kernel(along, place, own_ref, other_ref, *refs):
    weights, out_ref, data = refs[:SIDE], refs[SIDE], refs[SIDE + 1]
    deep = own_ref.shape[1]
    for core in range(CORES):

        @pl.when(place[2] == core)
        def _(core=core):
            both = (own_ref, other_ref) if core == 0 else (other_ref, own_ref)
            for n in range(SIDE):
                data[2 * n * deep : 2 * (n + 1) * deep, :] = jnp.concatenate([ref[n] for ref in both], axis=0)

    for k in range(SIDE):
        part = jnp.dot(weights[k][...], data[...], preferred_element_type=jnp.float32)
        out_ref[lax.rem(place[along] + SIDE - k, SIDE)] = part.astype(jnp.bfloat16)


def part_kernel(weights, data_ref, out_ref):
    out_ref[...] = jnp.dot(weights[...], data_ref[...], preferred_element_type=jnp.float32).astype(jnp.bfloat16)


def sent_parts_kernel(place, own_ref, other_ref, *refs):
    weights, data_ref, out_refs = refs[: SIDE - 1], refs[SIDE - 1], refs[SIDE:]
    deep = own_ref.shape[1]
    for core in range(CORES):

        @pl.when(place[2] == core)
        def _(core=core):
            both = (own_ref, other_ref) if core == 0 else (other_ref, own_ref)
            for n in range(SIDE):
                data_ref[2 * n * deep : 2 * (n + 1) * deep, :] = jnp.concatenate([ref[n] for ref in both], axis=0)

    for block, out_ref in zip(weights, out_refs):
        part_kernel(block, data_ref, out_ref)


def added(in_ref):
    total = in_ref[0].astype(jnp.float32)
    for n in range(1, in_ref.shape[0]):
        total = total + in_ref[n].astype(jnp.float32)
    return total


def gate_kernel(in_ref, gate_ref, out_ref):
    out_ref[...] = (added(in_ref) * gate_ref[...].astype(jnp.float32)).astype(jnp.bfloat16)


def pack_kernel(*refs):
    in_refs, out_ref = refs[:-1], refs[-1]
    shards, chunk, _ = out_ref.shape
    total = in_refs[0][...].astype(jnp.float32)
    for ref in in_refs[1:]:
        total = total + ref[...].astype(jnp.float32)
    piece, _ = pieces((1, LANES))
    lane = iota((1, LANES), 1)
    for s in range(shards):
        b, low = divmod(s * CAPACITY, LANES)
        block = jnp.zeros((chunk, LANES), jnp.float32)
        for q in range(PIECES):
            rows = total[q * chunk : (q + 1) * chunk]
            part = rows[:, b * LANES : (b + 1) * LANES]
            if low + CAPACITY > LANES:
                part = jnp.where(lane >= low, part, rows[:, (b + 1) * LANES : (b + 2) * LANES])
            turn = (q * CAPACITY - low) % LANES
            block = jnp.where(piece == q, pltpu.roll(part, turn, 1) if turn else part, block)
        out_ref[s] = block.astype(jnp.bfloat16)


def combine_kernel(in_ref, slot_ref, out_ref, spread, picks):
    piece, _ = pieces((1, LANES))
    held = held_slots(slot_ref.shape[1])
    chunk = in_ref.shape[1]
    for e in range(in_ref.shape[0]):
        block = in_ref[e].astype(jnp.float32)
        lanes = slice(e * LANES, (e + 1) * LANES)
        for q in range(PIECES):
            spread[q * chunk : (q + 1) * chunk, lanes] = jnp.where(piece == q, block, 0.0).astype(jnp.bfloat16)
        picks[lanes, :] = jnp.where(slot_ref[e : e + 1, :] == held, 1.0, 0.0).astype(jnp.bfloat16)
    out_ref[...] = jnp.dot(spread[...], picks[...], preferred_element_type=jnp.float32).astype(jnp.bfloat16)


def here():
    me = lax.axis_index("dp")
    return me // (SIDE * CORES), lax.rem(me // CORES, SIDE), lax.rem(me, CORES)


def column_copies(ks, in_ref, held, sems):
    wide = in_ref.shape[1] // (SIDE * SIDE)
    copies = []
    for to, k in zip(held, ks):
        for n in range(SIDE):
            block = n * SIDE + lax.rem(here()[1] + k, SIDE)
            columns = pl.ds(pl.multiple_of(block * wide, wide), wide)
            sem = sems.at[len(copies)]
            copies.append(pltpu.make_async_copy(in_ref.at[:, columns], to.at[:, pl.ds(n * wide, wide)], sem))
    return copies


def first_kernel(lengths, routes_ref, probs_ref, grad_ref, weights, out_ref, slot_ref, *refs):
    parts, held, (into, out_of) = refs[: SIDE - 1], refs[SIDE - 1 : -2], refs[-2:]
    taken = column_copies(FIRST, weights, held, into)
    given = [pltpu.make_async_copy(held[i], parts[i], out_of.at[i]) for i in range(SIDE - 1)]
    for copy in taken:
        copy.start()

    def pass_on(expert):
        i = expert // SIDE - 1
        if expert % SIDE == 0 and i >= 0:
            for copy in taken[i * SIDE : (i + 1) * SIDE]:
                copy.wait()
            given[i].start()

    dispatch_kernel(lengths, routes_ref, probs_ref, grad_ref, out_ref, slot_ref, pass_on)
    for copy in given:
        copy.wait()


def cut_up_kernel(up_ref, down_ref, *refs):
    out_refs, (kept_ref, windows, held, kept, fetched, out_of, into, kept_out) = refs[:SIDE], refs[SIDE:]
    wide, window = held.shape[2], windows.shape[2]
    fetches = []
    for n in range(SIDE):
        columns = pl.ds(n * wide // LANES * LANES, window)
        fetches.append(pltpu.make_async_copy(up_ref.at[:, columns], windows.at[n], fetched.at[n]))
    taken = column_copies((0,), down_ref, (kept,), into)
    for copy in fetches + taken:
        copy.start()
    given = [[pltpu.make_async_copy(held.at[n], ref, out_of.at[n]) for ref in out_refs] for n in range(SIDE)]

    def given_on(n, act):
        for k in range(SIDE):

            @pl.when(lax.rem(here()[0] + k, SIDE) == n)
            def _(k=k):
                act(given[n][k])

    for n in range(SIDE):
        fetches[n].wait()
        skip = n * wide % LANES
        held[n] = windows[n, :, skip : skip + wide]
        given_on(n, lambda copy: copy.start())
    for copy in taken:
        copy.wait()
    last = pltpu.make_async_copy(kept, kept_ref, kept_out)
    last.start()
    for n in range(SIDE):
        given_on(n, lambda copy: copy.wait())
    last.wait()


def send(part, dx, dy):
    return lax.ppermute(part, "dp", moves(dx, dy))


def product(along, place, rows, other, weights):
    _, deep, slots = rows.shape
    return call(
        functools.partial(product_kernel, along),
        jax.ShapeDtypeStruct((SIDE, weights[0].shape[0], slots), jnp.bfloat16),
        1,
        2 + SIDE,
        12 * MIB,
        [pltpu.VMEM((CORES * SIDE * deep, slots), jnp.bfloat16)],
    )(place, rows, other, *weights)


def on_device(grad_out, routes, probs, resp_len, w_down, w_up, gate_act):
    tokens, width = grad_out.shape
    hidden = w_down.shape[1]
    chunk = width // PIECES
    place = jnp.stack(here()).astype(jnp.int32)

    def half(*shape):
        return jax.ShapeDtypeStruct(shape, jnp.bfloat16)

    together = lax.optimization_barrier
    in_smem, in_vmem, in_hbm = (pl.BlockSpec(memory_space=m) for m in (pltpu.SMEM, pltpu.VMEM, pltpu.HBM))
    deep, features = w_down.shape[1:]
    part = half(deep, features // SIDE)
    outgoing, slots, *down = pl.pallas_call(
        first_kernel,
        out_shape=[half(EXPERTS, chunk, LANES), jax.ShapeDtypeStruct((EXPERTS, tokens), jnp.float32)]
        + [part] * (SIDE - 1),
        in_specs=[in_smem] + [in_vmem] * 3 + [in_hbm],
        out_specs=[in_vmem] * 2 + [in_hbm] * (SIDE - 1),
        scratch_shapes=[pltpu.VMEM(part.shape, part.dtype)] * (SIDE - 1)
        + [pltpu.SemaphoreType.DMA(((SIDE - 1) * SIDE,)), pltpu.SemaphoreType.DMA((SIDE - 1,))],
        compiler_params=pltpu.CompilerParams(vmem_limit_bytes=MOST),
    )(resp_len, routes.T, probs.T, grad_out.T, w_down[0])

    arrived = lax.all_to_all(outgoing, "expert", 0, 0, tiled=True)
    spread = call(unpack_kernel, half(width, SLOTS), 0, 1)(arrived)
    rows = gather(spread, X_GROUPS)
    rows, *down = together((rows, *[send(cut, 0, k) for k, cut in zip(FIRST, down)]))

    up_part = half(width, w_up.shape[2] // SIDE)
    window = -(-(up_part.shape[1] + LANES // 2) // LANES) * LANES
    *up, kept = pl.pallas_call(
        cut_up_kernel,
        out_shape=[up_part] * SIDE + [part],
        in_specs=[in_hbm] * 2,
        out_specs=[in_hbm] * (SIDE + 1),
        scratch_shapes=[
            pltpu.VMEM((SIDE, width, window), w_up.dtype),
            pltpu.VMEM((SIDE, *up_part.shape), w_up.dtype),
            pltpu.VMEM(part.shape, part.dtype),
        ]
        + [pltpu.SemaphoreType.DMA((SIDE,))] * 3
        + [pltpu.SemaphoreType.DMA],
        compiler_params=pltpu.CompilerParams(vmem_limit_bytes=MOST),
    )(after(w_up[0], rows), w_down[0])
    down = dict(zip(FIRST, down))
    partial = product(1, place, rows, lax.ppermute(rows, "dp", OTHER_CORE), [kept, *[down[k] for k in range(1, SIDE)]])

    partial, up = together((partial, up))
    spread = call(gate_kernel, half(hidden, SLOTS), 0, 2)(exchange(partial, Y_GROUPS), gate_act[0].T)
    rows = gather(spread, Y_GROUPS)
    rows, *sent = together((rows, *[send(up[k], k, 0) for k in FIRST]))
    up = [up[0]] + [sent[FIRST.index(k)] for k in range(1, SIDE)]
    other = lax.ppermute(rows, "dp", OTHER_CORE)
    depth = CORES * SIDE * hidden
    cost = dict(flops=2 * width * depth * SLOTS, moved=2 * depth * (width + SLOTS))
    data, *parts = call(sent_parts_kernel, [half(depth, SLOTS)] + [half(width, SLOTS)] * (SIDE - 1), 1, 1 + SIDE, 16 * MIB, **cost)(
        place, rows, other, *[up[k] for k in FIRST]
    )
    sums = [send(sent_part, -k, 0) for k, sent_part in zip(FIRST, parts)]
    sums.append(call(part_kernel, half(width, SLOTS), 0, 2, **cost)(up[0], data))
    returning = call(pack_kernel, half(EXPERTS, chunk, LANES), 0, SIDE)(*sums)
    back = lax.all_to_all(returning, "expert", 0, 0, tiled=True)
    scratch = [pltpu.VMEM((width, EXPERTS * LANES), jnp.bfloat16), pltpu.VMEM((EXPERTS * LANES, tokens), jnp.bfloat16)]
    return call(combine_kernel, half(width, tokens), 0, 2, scratch=scratch)(back, slots).T


def solution(mesh):
    in_specs = (
        P("expert", "dp"),
        P("expert", None),
        P("expert", None),
        P("expert", None),
        P("expert", "dp", None),
        P("expert", "dp", None),
        P("expert", None, "dp"),
    )
    out_specs = P("expert", "dp")
    return jax.shard_map(
        on_device, mesh=mesh, in_specs=in_specs, out_specs=out_specs, check_vma=False
    )
```
